32 devices in a mesh: dp: 8 (over y, x, core), mp: 4 (over z).
Axes of the slice: x: 2, y: 2, z: 4, core: 2. Of those that a mesh axis runs over, the one named last changes fastest.
Arguments:
- grad_square: bfloat16 [8, 3, 64, 8192], P('dp', None, None, 'mp'), may hold values from -6 to 6
- grad_narrow: bfloat16 [8, 2, 64, 1024], P('dp', None, None, 'mp'), may hold values from -6 to 6
- grad_wide: bfloat16 [8, 2, 64, 28672], P('dp', None, None, 'mp'), may hold values from -6 to 6
- error_square: float32 [8, 3, 64, 8192], P('dp', None, None, 'mp'), may hold values from -4 to 4
- error_narrow: float32 [8, 2, 64, 1024], P('dp', None, None, 'mp'), may hold values from -4 to 4
- error_wide: float32 [8, 2, 64, 28672], P('dp', None, None, 'mp'), may hold values from -4 to 4
- basis_square: float32 [3, 8192, 32], P(None, 'mp'), may hold values from -0.0625 to 0.0625
- basis_narrow: float32 [2, 1024, 32], P(None, 'mp'), may hold values from -0.1875 to 0.1875
- basis_wide: float32 [2, 28672, 32], P(None, 'mp'), may hold values from -0.03125 to 0.03125
Outputs:
- new_error_square: float32 [8, 3, 64, 8192], P('dp', None, None, 'mp')
- new_error_narrow: float32 [8, 2, 64, 1024], P('dp', None, None, 'mp')
- new_error_wide: float32 [8, 2, 64, 28672], P('dp', None, None, 'mp')
- new_basis_square: float32 [3, 8192, 32], P(None, 'mp')
- new_basis_narrow: float32 [2, 1024, 32], P(None, 'mp')
- new_basis_wide: float32 [2, 28672, 32], P(None, 'mp')
- left_basis: float32 [7, 64, 32], replicated
The draws below stay inside these ranges and needn't reach their ends.
All inputs are finite; a program needn't handle non-finite values.
Results may differ from the reference program's by a relative error of at most 0.0003.
Values sent between devices are 32-bit elements; how exact they have to be, the bound alone decides.
No kernel may reach another device: no remote copies, remote signals or barrier semaphores. Data moves between devices by JAX's collectives and lax.ppermute only.
A program may use at most 64 MiB of HBM per device.

```python
import jax
import jax.numpy as jnp
from jax import lax

D = 8192
KVW = 1024
FF = 28672
RANK = 32
ROWS = 64
REPLICAS = 8


def shard_levels(key, dims, split, least, high):
    def one(axis_at, blocks):
        heights = jax.random.uniform(jax.random.fold_in(jax.random.fold_in(key, 6), axis_at), (blocks,), jnp.float32, least / len(split), high / len(split))
        return jnp.repeat(jnp.exp(heights), dims[axis_at] // blocks).reshape((-1,) + (1,) * (len(dims) - axis_at - 1))

    level = one(*split[0])
    for cut in split[1:]:
        level = level * one(*cut)
    return level


def bell_draw(key, shape, spread, most, shards=(), dtype=jnp.bfloat16):
    drawn = jax.random.normal(key, shape, jnp.float32) * spread
    if len(shards) > 0:
        drawn = shard_levels(key, shape, shards, -0.22, 0.18) * drawn
    return jnp.clip(drawn, min=-most, max=most).astype(dtype)


def setup_inputs(seed: int = 0) -> dict:
    keys = jax.random.split(jax.random.key(seed), 10)
    grad_square = bell_draw(keys[0], (REPLICAS, 3, ROWS, D), 1.0, 6.0, ((0, 8), (3, 4)))
    grad_narrow = bell_draw(keys[1], (REPLICAS, 2, ROWS, KVW), 1.0, 6.0, ((0, 8), (3, 4)))
    grad_wide = bell_draw(keys[2], (REPLICAS, 2, ROWS, FF), 1.0, 6.0, ((0, 8), (3, 4)))
    error_square = bell_draw(keys[3], (REPLICAS, 3, ROWS, D), 0.5, 4.0, ((0, 8), (3, 4)), jnp.float32)
    error_narrow = bell_draw(keys[4], (REPLICAS, 2, ROWS, KVW), 0.5, 4.0, ((0, 8), (3, 4)), jnp.float32)
    error_wide = bell_draw(keys[5], (REPLICAS, 2, ROWS, FF), 0.5, 4.0, ((0, 8), (3, 4)), jnp.float32)
    basis_square = bell_draw(keys[6], (3, D, RANK), D ** -0.5, 0.0625, ((1, 4),), jnp.float32)
    basis_narrow = bell_draw(keys[7], (2, KVW, RANK), KVW ** -0.5, 0.1875, ((1, 4),), jnp.float32)
    basis_wide = bell_draw(keys[8], (2, FF, RANK), FF ** -0.5, 0.03125, ((1, 4),), jnp.float32)
    return {"grad_square": grad_square, "grad_narrow": grad_narrow, "grad_wide": grad_wide, "error_square": error_square, "error_narrow": error_narrow, "error_wide": error_wide, "basis_square": basis_square, "basis_narrow": basis_narrow, "basis_wide": basis_wide}


def orthonormal(product):
    gram_matrix = jnp.einsum('mrk,mrl->mkl', product, product, precision=lax.Precision.HIGHEST)
    factor = jnp.linalg.cholesky(gram_matrix)

    def solve_one(lower_factor, rows):
        return jax.scipy.linalg.solve_triangular(lower_factor, rows.T, lower=True).T
    return jax.vmap(solve_one)(factor, product)

def reference(grad_square, grad_narrow, grad_wide, error_square, error_narrow, error_wide, basis_square, basis_narrow, basis_wide):
    groups = [(grad_square, error_square, basis_square), (grad_narrow, error_narrow, basis_narrow), (grad_wide, error_wide, basis_wide)]
    merged_all = []
    products = []
    for grad_part, error_part, basis_part in groups:
        merged = grad_part.astype(jnp.float32) + error_part
        merged_all.append(merged)
        products.append(jnp.einsum('nmrc,mck->mrk', merged, basis_part, precision=lax.Precision.HIGHEST))
    left_basis = orthonormal(jnp.concatenate(products, axis=0))
    starts = [0, 3, 5, 7]
    new_errors = []
    new_bases = []
    for index in range(3):
        left_part = left_basis[starts[index]:starts[index + 1]]
        merged = merged_all[index]
        new_basis = jnp.einsum('nmrc,mrk->mck', merged, left_part, precision=lax.Precision.HIGHEST)
        approx = jnp.einsum('mrk,mck->mrc', left_part, new_basis, precision=lax.Precision.HIGHEST)
        new_errors.append(merged - approx[None])
        new_bases.append(new_basis)
    return (new_errors[0], new_errors[1], new_errors[2], new_bases[0], new_bases[1], new_bases[2], left_basis)
```

```python
import functools
import math

import jax
import jax.numpy as jnp
from jax import lax
from jax.experimental import pallas as pl
from jax.experimental.pallas import tpu as pltpu
from jax.sharding import PartitionSpec as P

LANES = 128
MIB = 1024 * 1024
F32 = jnp.float32
BF16 = jnp.bfloat16


def round_up(value, step):
    return -(-value // step) * step


def chunk_of(columns, most=1024):
    if columns % LANES:
        return columns
    width = min(columns, most) // LANES * LANES
    while columns % width:
        width -= LANES
    return width


def split2(value):
    high = value.astype(BF16)
    low = (value - high.astype(F32)).astype(BF16)
    return high, low


def dot_last(left, right):
    return lax.dot_general(left, right, (((1,), (1,)), ((), ())), preferred_element_type=F32)


def dot_plain(left, right):
    return lax.dot_general(left, right, (((1,), (0,)), ((), ())), preferred_element_type=F32)


def lane_slice(column, width):
    if isinstance(column, int):
        return pl.ds(column, width)
    return pl.ds(pl.multiple_of(column, LANES), width)


class Layout:
    def __init__(self, groups, dp_bits):
        self.groups = groups
        self.places = []
        self.starts = []
        self.firsts = []
        used = 0
        matrices = 0
        for count, columns in groups:
            self.firsts.append(matrices)
            self.places.append(used)
            for _ in range(count):
                self.starts.append(used)
                used += round_up(columns, LANES)
            matrices += count
        self.matrices = matrices
        self.used = used
        unit = 1 << max(1, dp_bits - 2)
        units = max(4, -(-used // (2 * unit * LANES)))
        self.half = units * unit * LANES
        self.packed = 2 * self.half
        self.cells = []
        offset = 0
        base = units // 8
        shares = [2 * base + 2, 2 * base + 2, 2 * base, units - 6 * base - 4]
        if base == 0 or shares[3] < 1:
            shares = [units // 4] * 3 + [units - 3 * (units // 4)]
        for cell, share in enumerate(shares):
            width = share * unit * LANES
            self.cells.append((offset, width, cell % 2))
            offset += width
        self.orders = (list(range(1, dp_bits)), list(range(dp_bits - 1, 0, -1)))
        self.columns = sum(count * columns for count, columns in groups)

    def granule(self, cell):
        offset, width, _ = self.cells[cell]
        return math.gcd(*self.starts, self.half, offset, width // 2)

    def segments(self, low, high, most):
        found = []
        for index, (count, columns) in enumerate(self.groups):
            for matrix in range(count):
                place = self.places[index] + matrix * round_up(columns, LANES)
                begin, end = max(low, place), min(high, place + columns)
                if begin < end:
                    width = chunk_of(end - begin, most)
                    found.append((index, matrix, begin - place, begin, width, (end - begin) // width))
        return found


def widen(value):
    rows, width = value.shape
    if width % LANES == 0:
        return value
    return jnp.concatenate([value, jnp.zeros((rows, round_up(width, LANES) - width), value.dtype)], axis=1)


def bit_of(bit):
    return (lax.axis_index("dp") >> bit) & 1


def params(limit=8):
    return pltpu.CompilerParams(vmem_limit_bytes=limit * MIB)


VMEM_SPEC = pl.BlockSpec(memory_space=pltpu.VMEM)
HBM_SPEC = pl.BlockSpec(memory_space=pltpu.HBM)


def in_hbm(values):
    return [pltpu.with_memory_space_constraint(value, pltpu.HBM) for value in values]


def odd_buffer(layout, rows):
    odd = [(count, columns) for count, columns in layout.groups if columns % LANES] or [(1, LANES)]
    return pltpu.VMEM((max(count for count, _ in odd), rows, max(columns for _, columns in odd)), F32)


def merge_and_project_kernel(layout, grad_refs, error_refs, basis_refs, merged_ref, send_ref, keep_ref, grad_bufs, basis_bufs, odd_ref, total, sems):
    rank = total.shape[1] // 2
    rows = total.shape[2] // 2
    plans = []
    slot = 0
    for segment in layout.segments(0, layout.used, 2048):
        plans.append((*segment, slot))
        slot += segment[-1]

    def copies_of(plan, at):
        index, matrix, column, place, width, _, base = plan
        where = (matrix, slice(None), lane_slice(column + at * width, width))
        error_to = odd_ref.at[matrix] if width % LANES else merged_ref.at[:, lane_slice(place + at * width, width)]
        return (
            pltpu.make_async_copy(grad_refs[index].at[(0,) + where], grad_bufs[index].at[where], sems.at[0, base + at]),
            pltpu.make_async_copy(error_refs[index].at[(0,) + where], error_to, sems.at[1, base + at]),
            pltpu.make_async_copy(basis_refs[index].at[where], basis_bufs[index].at[where], sems.at[2, base + at]),
        )

    for plan in plans:
        for at in range(plan[5]):
            for copy in copies_of(plan, at):
                copy.start()
    if layout.used < layout.packed:
        merged_ref[:, layout.used :] = jnp.zeros((rows, layout.packed - layout.used), F32)
    total[...] = jnp.zeros_like(total)
    for plan in plans:
        index, matrix, column, place, width, steps, _ = plan

        def body(at, carry, plan=plan, index=index, matrix=matrix, column=column, place=place, width=width):
            for copy in copies_of(plan, at):
                copy.wait()
            where = (matrix, slice(None), lane_slice(column + at * width, width))
            packed = (slice(None), lane_slice(place + at * width, round_up(width, LANES)))
            error = odd_ref[matrix] if width % LANES else merged_ref[packed]
            merged = error + grad_bufs[index][where].astype(F32)
            merged_ref[packed] = widen(merged)
            merged_parts = jnp.concatenate(split2(merged), axis=0)
            basis_parts = jnp.concatenate(split2(basis_bufs[index][where]), axis=0)
            total[layout.firsts[index] + matrix] += dot_last(basis_parts, merged_parts)
            return carry

        if steps == 1:
            body(0, 0)
        else:
            lax.fori_loop(0, steps, body, 0)
    core = bit_of(0)
    quarter = rank // 4
    for matrix in range(total.shape[0]):
        value = total[matrix]
        top = value[:rank, :rows] + value[:rank, rows:]
        top = top + (value[rank:, :rows] + value[rank:, rows:])
        quarters = [top[number * quarter : (number + 1) * quarter] for number in range(4)]
        halves = [jnp.concatenate(quarters[2 * half : 2 * half + 2], axis=1) for half in range(2)]
        send_ref[matrix] = jnp.where(core == 0, halves[1], halves[0])
        keep_ref[matrix] = jnp.where(core == 0, halves[0], halves[1])


def merge_and_project(layout, rank, rows, grads, errors, bases):
    def kernel(*refs):
        merge_and_project_kernel(layout, refs[0:3], refs[3:6], refs[6:9], *refs[9:12], refs[12:15], refs[15:18], *refs[18:])

    read = sum(value.size * value.dtype.itemsize for value in (*grads, *errors, *bases))
    slots = sum(segment[-1] for segment in layout.segments(0, layout.used, 2048))
    return pl.pallas_call(
        kernel,
        name="merge_and_project",
        out_shape=[pltpu.VMEM((rows, layout.packed), F32)]
        + [jax.ShapeDtypeStruct((layout.matrices, rank // 4, 2 * rows), F32)] * 2,
        in_specs=[HBM_SPEC] * 9,
        out_specs=[VMEM_SPEC] * 3,
        scratch_shapes=[pltpu.VMEM((count, rows, columns), BF16) for count, columns in layout.groups]
        + [pltpu.VMEM((count, rank, columns), F32) for count, columns in layout.groups]
        + [
            odd_buffer(layout, rows),
            pltpu.VMEM((layout.matrices, 2 * rank, 2 * rows), F32),
            pltpu.SemaphoreType.DMA((3, slots)),
        ],
        compiler_params=params(12),
        cost_estimate=pl.CostEstimate(flops=8 * rows * rank * layout.columns, bytes_accessed=read, transcendentals=0),
    )(*in_hbm(grads), *in_hbm(errors), *in_hbm(bases))


def take_half(layout, merged):
    def kernel(merged_ref, out_ref):
        out_ref[...] = merged_ref[:, lane_slice((1 - bit_of(0)) * layout.half, layout.half)]

    return add_call("take_half", kernel, [(merged.shape[0], layout.half)], [merged])[0]


def split_sum(layout, merged, received):
    rows = merged.shape[0]

    def kernel(merged_ref, received_ref, out_ref):
        own = bit_of(0) * layout.half
        total = merged_ref[:, lane_slice(own, layout.half)] + received_ref[...]
        out_ref[:rows], out_ref[rows:] = split2(total)

    return pl.pallas_call(
        kernel,
        name="split_sum",
        out_shape=jax.ShapeDtypeStruct((2 * rows, layout.half), BF16),
        in_specs=[VMEM_SPEC] * 2,
        out_specs=VMEM_SPEC,
        compiler_params=params(),
        cost_estimate=pl.CostEstimate(flops=rows * layout.half, bytes_accessed=1_000_000, transcendentals=0),
    )(merged, received)


def next_sum_kernel(layout, step, *refs):
    for part in range(2):
        kept_ref, received_ref = refs[2 * part : 2 * part + 2]
        width = kept_ref.shape[1] // 2
        which = bit_of(layout.orders[part][step])
        for out_ref, pick in zip(refs[4 + 2 * part : 6 + 2 * part], (1 - which, which)):
            where = (slice(None), lane_slice(pick * width, width))
            out_ref[...] = kept_ref[where] + received_ref[where]


def next_sum(layout, step, arrays):
    rows = arrays[0].shape[0]
    return pl.pallas_call(
        functools.partial(next_sum_kernel, layout, step),
        name="next_sum",
        out_shape=[jax.ShapeDtypeStruct((rows, arrays[2 * part].shape[1] // 2), F32) for part in range(2) for _ in range(2)],
        in_specs=[VMEM_SPEC] * 4,
        out_specs=[VMEM_SPEC] * 4,
        compiler_params=params(),
        cost_estimate=pl.CostEstimate(flops=rows * layout.half, bytes_accessed=1_000_000, transcendentals=0),
    )(*arrays)


def add_call(name, kernel, out_shapes, arrays):
    return pl.pallas_call(
        kernel,
        name=name,
        out_shape=[jax.ShapeDtypeStruct(shape, F32) for shape in out_shapes],
        in_specs=[VMEM_SPEC] * len(arrays),
        out_specs=[VMEM_SPEC] * len(out_shapes),
        compiler_params=params(),
        cost_estimate=pl.CostEstimate(
            flops=sum(rows * columns for rows, columns in out_shapes), bytes_accessed=1_000_000, transcendentals=0
        ),
    )(*arrays)


def last_sum(arrays):
    def kernel(*refs):
        for part in range(2):
            refs[4 + part][...] = refs[2 * part][...] + refs[2 * part + 1][...]

    return add_call("last_sum", kernel, [arrays[0].shape, arrays[2].shape], arrays)


def join(layout, step, pieces, received):
    shapes = [(piece.shape[0], 2 * piece.shape[1]) for piece in pieces]

    def kernel(*refs):
        for part in range(2):
            which = bit_of(layout.orders[part][step])
            width = refs[part].shape[1]
            refs[4 + part][:, lane_slice(which * width, width)] = refs[part][...]
            refs[4 + part][:, lane_slice((1 - which) * width, width)] = refs[2 + part][...]

    return add_call("join", kernel, shapes, (*pieces, *received))


def pack(blocks):
    def kernel(*refs):
        column = 0
        for ref in refs[:-1]:
            refs[-1][:, column : column + ref.shape[1]] = ref[...]
            column += ref.shape[1]

    shape = (blocks[0].shape[0], sum(block.shape[1] for block in blocks))
    return add_call("pack", kernel, [shape], blocks)[0]


def orthonormal_rows(product_t, block=4):
    matrices, rank, rows = product_t.shape
    gram = jnp.stack(
        [
            lax.dot_general(
                product_t[j], product_t[j], (((1,), (1,)), ((), ())), precision=lax.Precision.HIGHEST, preferred_element_type=F32
            )
            for j in range(matrices)
        ]
    )
    filler = jnp.zeros((matrices, rank, LANES - rank - rows), F32)
    work = jnp.concatenate([gram, filler, product_t], axis=2)
    done = []
    for first in range(0, rank, block):
        start = first % 8
        row_id = lax.broadcasted_iota(jnp.int32, (1, work.shape[1], 1), 1)
        columns = [jnp.broadcast_to(work[:, :, first + t : first + t + 1], work.shape) for t in range(block)]
        pivot_rows = [work[:, start + t : start + t + 1, :] for t in range(block)]
        scaled = []
        for t in range(block):
            at = start + t
            inverse = 1.0 / columns[t][:, at : at + 1, :]
            scaled.append(pivot_rows[t] * inverse)
            for s in range(t + 1, block):
                pivot_rows[s] = pivot_rows[s] - scaled[t] * columns[t][:, start + s : start + s + 1, :]
                columns[s] = columns[s] - columns[t] * (columns[s][:, at : at + 1, :] * inverse)
        change = columns[0] * scaled[0]
        for t in range(1, block):
            change = change + columns[t] * scaled[t]
        work = work - jnp.where(row_id >= start + block, change, 0.0)
        for t in range(block):
            work = jnp.where(row_id == start + t, pivot_rows[t], work)
        if start + block == 8:
            done.append(work[:, :8, :])
            work = work[:, 8:, :]
    work = jnp.concatenate(done, axis=1)
    row_id = lax.broadcasted_iota(jnp.int32, work.shape, 1)
    lane_id = lax.broadcasted_iota(jnp.int32, work.shape, 2)
    pivots = jnp.sum(jnp.where(row_id == lane_id, work, 0.0), axis=2, keepdims=True)
    return work[:, :, LANES - rows :] * (1.0 / jnp.sqrt(pivots))


def factor_kernel(layout, own_ref, other_ref, sums_ref, left_ref, *refs):
    outs, parts_ref = refs[:-1], refs[-1]
    rows = left_ref.shape[2]
    core = bit_of(0)
    own, other = (jnp.concatenate([ref[:, :, :rows], ref[:, :, rows:]], axis=1) for ref in (own_ref, other_ref))
    both = [jnp.where(core == 0, one, two) for one, two in ((own, other), (other, own))]
    left = orthonormal_rows(jnp.concatenate(both, axis=1))
    left_ref[...] = left
    high, low = split2(left)
    parts_ref[...] = jnp.concatenate([high, high, low], axis=2)
    for cell, (offset, width, part) in enumerate(layout.cells):
        which = bit_of(layout.orders[part][0])
        width //= 2
        for out_ref, pick in zip(outs[2 * cell : 2 * cell + 2], (1 - which, which)):
            begin = offset + pick * width
            for at in range(0, width, layout.granule(cell)):
                column = core * layout.half + begin + at
                matrix = sum((column >= start).astype(jnp.int32) for start in layout.starts[1:])
                value = sums_ref[:, lane_slice(begin + at, layout.granule(cell))]
                stacked = jnp.concatenate([value, value[:rows]], axis=0)
                out_ref[:, at : at + layout.granule(cell)] = dot_plain(parts_ref[matrix], stacked)


def factor(layout, rank, rows, own, other, sums):
    return pl.pallas_call(
        functools.partial(factor_kernel, layout),
        name="factor",
        out_shape=[jax.ShapeDtypeStruct((layout.matrices, rank, rows), F32)]
        + [jax.ShapeDtypeStruct((rank, width // 2), F32) for _, width, _ in layout.cells for _ in range(2)],
        in_specs=[VMEM_SPEC] * 3,
        out_specs=[VMEM_SPEC] * (1 + 2 * len(layout.cells)),
        scratch_shapes=[pltpu.VMEM((layout.matrices, rank, 3 * rows), BF16)],
        compiler_params=params(),
        cost_estimate=pl.CostEstimate(flops=8 * rows * rank * layout.half, bytes_accessed=10_000_000, transcendentals=0),
    )(own, other, sums)


def turn(left):
    matrices, rank, rows = left.shape

    def kernel(left_ref, out_ref):
        high, low = split2(left_ref[...])
        for j in range(matrices):
            parts = jnp.concatenate([high[j], high[j], low[j]], axis=0).astype(F32)
            out_ref[j] = parts.T.astype(BF16)

    return pl.pallas_call(
        kernel,
        name="turn",
        out_shape=pltpu.VMEM((matrices, rows, 3 * rank), BF16),
        in_specs=[VMEM_SPEC],
        out_specs=VMEM_SPEC,
        compiler_params=params(),
        cost_estimate=pl.CostEstimate(flops=100_000, bytes_accessed=100_000, transcendentals=0),
    )(left)


def update_kernel(layout, stage, turned_ref, merged_ref, right_refs, error_refs, basis_refs, right_buf, error_buf, odd_error, odd_basis, sems):
    core = bit_of(0)
    ends = []
    slot = 0
    for half_core in range(2):
        for offset, width, part in layout.cells:
            size = width // 2
            for number in range(2):
                low = half_core * layout.half + offset + number * size
                segments = layout.segments(low, low + size, 4096)
                shift = offset // 2 - low
                named = bit_of(layout.orders[part][0]) == number
                if stage == 2:
                    mine = core != half_core
                else:
                    mine = (core == half_core) & (named if stage == 0 else ~named)

                def copies_of(segment, base, at):
                    index, matrix, column, place, width, _ = segment
                    where = (matrix, slice(None), lane_slice(column + at * width, width))
                    packed = (slice(None), lane_slice(place + at * width, width))
                    odd = width % LANES
                    error_from = odd_error.at[matrix] if odd else error_buf.at[packed]
                    basis_from = odd_basis.at[matrix] if odd else right_buf.at[packed]
                    return (
                        pltpu.make_async_copy(error_from, error_refs[index].at[(0,) + where], sems.at[0, base + at]),
                        pltpu.make_async_copy(basis_from, basis_refs[index].at[where], sems.at[1, base + at]),
                    )

                def run(segments=segments, base=slot, named=named, shift=shift, copies_of=copies_of):
                    for segment in segments:
                        index, matrix, _, place, width, steps = segment
                        padded = round_up(width, LANES)

                        def body(at, carry, segment=segment, base=base, index=index, matrix=matrix, place=place, width=width, padded=padded):
                            source = (slice(None), lane_slice(place + shift + at * width, padded))
                            packed = (slice(None), lane_slice(place + at * width, padded))
                            right = right_refs[0][source]
                            if stage == 2:
                                right = jnp.where(named, right, right_refs[1][source])
                            right_buf[packed] = right
                            high, low = split2(right)
                            turned = turned_ref[layout.firsts[index] + matrix]
                            approx = dot_plain(turned, jnp.concatenate([high, low, high], axis=0))
                            error = merged_ref[packed] - approx
                            error_buf[packed] = error
                            if width < padded:
                                odd_error[matrix] = error[:, :width]
                                odd_basis[matrix] = right[:, :width]
                            for copy in copies_of(segment, base, at):
                                copy.start()
                            return carry

                        if steps == 1:
                            body(0, 0)
                        else:
                            lax.fori_loop(0, steps, body, 0)
                        base += steps

                def end(segments=segments, base=slot, copies_of=copies_of):
                    for segment in segments:
                        for at in range(segment[-1]):
                            for copy in copies_of(segment, base, at):
                                copy.wait()
                        base += segment[-1]

                pl.when(mine)(run)
                ends.append((mine, end))
                slot += sum(segment[-1] for segment in segments)
    for mine, end in ends:
        pl.when(mine)(end)


def update_error(layout, rank, stage, turned, merged, rights, before=()):
    rows = merged.shape[0]
    groups = len(layout.groups)
    ins = 2 + len(rights)

    def kernel(*refs):
        turned_ref, merged_ref, *right_refs = refs[:ins]
        refs = refs[ins + len(before) :]
        update_kernel(layout, stage, turned_ref, merged_ref, right_refs, refs[:groups], refs[groups : 2 * groups], *refs[2 * groups :])

    slots = 0
    for low in range(0, layout.packed, layout.half):
        for offset, width, _ in layout.cells:
            for begin in (low + offset, low + offset + width // 2):
                slots += sum(segment[-1] for segment in layout.segments(begin, begin + width // 2, 4096))
    return pl.pallas_call(
        kernel,
        name="update_" + ("first", "own", "other")[stage],
        out_shape=[jax.ShapeDtypeStruct((1, count, rows, columns), F32) for count, columns in layout.groups]
        + [jax.ShapeDtypeStruct((count, rank, columns), F32) for count, columns in layout.groups],
        in_specs=[VMEM_SPEC] * ins + [HBM_SPEC] * len(before),
        out_specs=[HBM_SPEC] * (2 * groups),
        input_output_aliases={ins + number: number for number in range(len(before))},
        scratch_shapes=[
            pltpu.VMEM((rank, layout.packed), F32),
            pltpu.VMEM((rows, layout.packed), F32),
            odd_buffer(layout, rows),
            odd_buffer(layout, rank),
            pltpu.SemaphoreType.DMA((2, slots)),
        ],
        compiler_params=params(12),
        cost_estimate=pl.CostEstimate(flops=100_000, bytes_accessed=40_000_000 if stage else 100_000, transcendentals=0),
    )(turned, merged, *rights, *before)


def swap(value, axis, size, bit):
    return lax.ppermute(value, axis, [(i, i ^ (1 << bit)) for i in range(size)])


def sum_over_bits(value, axis, size, bits):
    while bits:
        turns = [0]
        for bit in bits[:2]:
            turns = turns + [turn | (1 << bit) for turn in turns]
        bits = bits[2:]
        terms = [value] + [lax.ppermute(value, axis, [(i, i ^ turn) for i in range(size)]) for turn in turns[1:]]
        while len(terms) > 1:
            terms = [one + two for one, two in zip(terms[::2], terms[1::2])]
        value = terms[0]
    return value


def per_device(sizes, grad_square, grad_narrow, grad_wide, error_square, error_narrow, error_wide, basis_square, basis_narrow, basis_wide):
    dp, mp = sizes
    dp_bits = dp.bit_length() - 1
    mp_bits = mp.bit_length() - 1
    grads = (grad_square, grad_narrow, grad_wide)
    errors = (error_square, error_narrow, error_wide)
    bases = tuple(jnp.swapaxes(value, 1, 2) for value in (basis_square, basis_narrow, basis_wide))
    rows = grad_square.shape[2]
    rank = basis_square.shape[2]
    layout = Layout([(value.shape[1], value.shape[3]) for value in grads], dp_bits)
    order = lax.optimization_barrier
    steps = dp_bits - 1

    def swap_parts(values, step):
        return [swap(values[part], "dp", dp, layout.orders[part][step]) for part in range(2)]

    merged, send, product = merge_and_project(layout, rank, rows, grads, errors, bases)
    product = product + swap(send, "dp", dp, 0)
    merged, product = order((merged, product))
    received = swap(take_half(layout, merged), "dp", dp, 0)
    product = sum_over_bits(product, "dp", dp, list(range(1, dp_bits)))
    product = sum_over_bits(product, "mp", mp, list(range(mp_bits)))
    received, product = order((received, product))
    sums = split_sum(layout, merged, received)
    left, *arrays = factor(layout, rank, rows, product, swap(product, "dp", dp, 0), sums)
    turned = turn(left)

    chunks = [arrays[4 * chunk : 4 * chunk + 4] for chunk in range(2)]
    for step in range(max(1, steps - 1)):
        traded = [swap_parts(chunk[::2], step) for chunk in chunks]
        chunks = [[chunk[1], one, chunk[3], two] for chunk, (one, two) in zip(chunks, traded)]
        if step < steps - 2:
            chunks = [next_sum(layout, step + 1, chunk) for chunk in chunks]
    chunks = [last_sum(chunk) for chunk in chunks]
    if steps > 1:
        traded = [swap_parts(chunk, steps - 1) for chunk in chunks]
        first = last_sum([chunks[0][0], traded[0][0], chunks[0][1], traded[0][1]])
        one, two = order((*traded[1], *first))[:2]
        chunks = [first, last_sum([chunks[1][0], one, chunks[1][1], two])]
    for step in reversed(range(1, steps - 1)):
        chunks = [join(layout, step, chunk, swap_parts(chunk, step)) for chunk in chunks]
    news = [swap_parts(chunk, 0) for chunk in chunks]
    own = pack([piece for chunk in chunks for piece in chunk])
    first_other = swap(own, "dp", dp, 0)
    outs = update_error(layout, rank, 0, turned, merged, [own])
    tied = order((*outs, *news[0], *news[1]))
    outs, own = tied[: len(outs)], pack(tied[len(outs) :])
    other = swap(own, "dp", dp, 0)
    outs = update_error(layout, rank, 1, turned, merged, [own], outs)
    outs = update_error(layout, rank, 2, turned, merged, [first_other, other], outs)
    return (*outs[:3], *(jnp.swapaxes(value, 1, 2) for value in outs[3:]), jnp.swapaxes(left, 1, 2))


def solution(mesh):
    in_specs = (P("dp", None, None, "mp"),) * 6 + (P(None, "mp", None),) * 3
    out_specs = (P("dp", None, None, "mp"),) * 3 + (P(None, "mp", None),) * 3 + (P(),)
    sizes = (mesh.shape["dp"], mesh.shape["mp"])
    return jax.shard_map(
        functools.partial(per_device, sizes), mesh=mesh, in_specs=in_specs, out_specs=out_specs, check_vma=False
    )
```

```python
import functools
import math

import jax
import jax.numpy as jnp
from jax import lax
from jax.experimental import pallas as pl
from jax.experimental.pallas import tpu as pltpu
from jax.sharding import PartitionSpec as P

LANES = 128
MIB = 1024 * 1024
F32 = jnp.float32
BF16 = jnp.bfloat16


def round_up(value, step):
    return -(-value // step) * step


def chunk_of(columns, most=1024):
    if columns % LANES:
        return columns
    width = min(columns, most) // LANES * LANES
    while columns % width:
        width -= LANES
    return width


def split2(value):
    high = value.astype(BF16)
    low = (value - high.astype(F32)).astype(BF16)
    return high, low


def dot_last(left, right):
    return lax.dot_general(left, right, (((1,), (1,)), ((), ())), preferred_element_type=F32)


def dot_plain(left, right):
    return lax.dot_general(left, right, (((1,), (0,)), ((), ())), preferred_element_type=F32)


def lane_slice(column, width):
    if isinstance(column, int):
        return pl.ds(column, width)
    return pl.ds(pl.multiple_of(column, LANES), width)


class Layout:
    def __init__(self, groups, dp_bits):
        self.groups = groups
        self.places = []
        self.starts = []
        self.firsts = []
        used = 0
        matrices = 0
        for count, columns in groups:
            self.firsts.append(matrices)
            self.places.append(used)
            for _ in range(count):
                self.starts.append(used)
                used += round_up(columns, LANES)
            matrices += count
        self.matrices = matrices
        self.used = used
        unit = 1 << max(1, dp_bits - 2)
        units = max(4, -(-used // (2 * unit * LANES)))
        self.half = units * unit * LANES
        self.packed = 2 * self.half
        self.cells = []
        offset = 0
        base = units // 8
        shares = [2 * base + 2, 2 * base + 2, 2 * base, units - 6 * base - 4]
        if base == 0 or shares[3] < 1:
            shares = [units // 4] * 3 + [units - 3 * (units // 4)]
        for cell, share in enumerate(shares):
            width = share * unit * LANES
            self.cells.append((offset, width, cell % 2))
            offset += width
        self.orders = (list(range(1, dp_bits)), list(range(dp_bits - 1, 0, -1)))
        self.columns = sum(count * columns for count, columns in groups)

    def granule(self, cell):
        offset, width, _ = self.cells[cell]
        return math.gcd(*self.starts, self.half, offset, width // 2)

    def segments(self, low, high, most):
        found = []
        for index, (count, columns) in enumerate(self.groups):
            for matrix in range(count):
                place = self.places[index] + matrix * round_up(columns, LANES)
                begin, end = max(low, place), min(high, place + columns)
                if begin < end:
                    width = chunk_of(end - begin, most)
                    found.append((index, matrix, begin - place, begin, width, (end - begin) // width))
        return found


def widen(value):
    rows, width = value.shape
    if width % LANES == 0:
        return value
    return jnp.concatenate([value, jnp.zeros((rows, round_up(width, LANES) - width), value.dtype)], axis=1)


def bit_of(bit):
    return (lax.axis_index("dp") >> bit) & 1


def params(limit=8):
    return pltpu.CompilerParams(vmem_limit_bytes=limit * MIB)


VMEM_SPEC = pl.BlockSpec(memory_space=pltpu.VMEM)
HBM_SPEC = pl.BlockSpec(memory_space=pltpu.HBM)


def in_hbm(values):
    return [pltpu.with_memory_space_constraint(value, pltpu.HBM) for value in values]


def odd_buffer(layout, rows):
    odd = [(count, columns) for count, columns in layout.groups if columns % LANES] or [(1, LANES)]
    return pltpu.VMEM((max(count for count, _ in odd), rows, max(columns for _, columns in odd)), F32)


def merge_and_project_kernel(layout, grad_refs, error_refs, basis_refs, merged_ref, send_ref, keep_ref, grad_bufs, basis_bufs, odd_ref, total, sems):
    rank = total.shape[1] // 2
    rows = total.shape[2] // 2
    plans = []
    slot = 0
    for segment in layout.segments(0, layout.used, 2048):
        plans.append((*segment, slot))
        slot += segment[-1]

    def copies_of(plan, at):
        index, matrix, column, place, width, _, base = plan
        where = (matrix, slice(None), lane_slice(column + at * width, width))
        error_to = odd_ref.at[matrix] if width % LANES else merged_ref.at[:, lane_slice(place + at * width, width)]
        return (
            pltpu.make_async_copy(grad_refs[index].at[(0,) + where], grad_bufs[index].at[where], sems.at[0, base + at]),
            pltpu.make_async_copy(error_refs[index].at[(0,) + where], error_to, sems.at[1, base + at]),
            pltpu.make_async_copy(basis_refs[index].at[where], basis_bufs[index].at[where], sems.at[2, base + at]),
        )

    for plan in plans:
        for at in range(plan[5]):
            for copy in copies_of(plan, at):
                copy.start()
    if layout.used < layout.packed:
        merged_ref[:, layout.used :] = jnp.zeros((rows, layout.packed - layout.used), F32)
    total[...] = jnp.zeros_like(total)
    for plan in plans:
        index, matrix, column, place, width, steps, _ = plan

        def body(at, carry, plan=plan, index=index, matrix=matrix, column=column, place=place, width=width):
            for copy in copies_of(plan, at):
                copy.wait()
            where = (matrix, slice(None), lane_slice(column + at * width, width))
            packed = (slice(None), lane_slice(place + at * width, round_up(width, LANES)))
            error = odd_ref[matrix] if width % LANES else merged_ref[packed]
            merged = error + grad_bufs[index][where].astype(F32)
            merged_ref[packed] = widen(merged)
            merged_parts = jnp.concatenate(split2(merged), axis=0)
            basis_parts = jnp.concatenate(split2(basis_bufs[index][where]), axis=0)
            total[layout.firsts[index] + matrix] += dot_last(basis_parts, merged_parts)
            return carry

        if steps == 1:
            body(0, 0)
        else:
            lax.fori_loop(0, steps, body, 0)
    core = bit_of(0)
    quarter = rank // 4
    for matrix in range(total.shape[0]):
        value = total[matrix]
        top = value[:rank, :rows] + value[:rank, rows:]
        top = top + (value[rank:, :rows] + value[rank:, rows:])
        quarters = [top[number * quarter : (number + 1) * quarter] for number in range(4)]
        halves = [jnp.concatenate(quarters[2 * half : 2 * half + 2], axis=1) for half in range(2)]
        send_ref[matrix] = jnp.where(core == 0, halves[1], halves[0])
        keep_ref[matrix] = jnp.where(core == 0, halves[0], halves[1])


def merge_and_project(layout, rank, rows, grads, errors, bases):
    def kernel(*refs):
        merge_and_project_kernel(layout, refs[0:3], refs[3:6], refs[6:9], *refs[9:12], refs[12:15], refs[15:18], *refs[18:])

    read = sum(value.size * value.dtype.itemsize for value in (*grads, *errors, *bases))
    slots = sum(segment[-1] for segment in layout.segments(0, layout.used, 2048))
    return pl.pallas_call(
        kernel,
        name="merge_and_project",
        out_shape=[pltpu.VMEM((rows, layout.packed), F32)]
        + [jax.ShapeDtypeStruct((layout.matrices, rank // 4, 2 * rows), F32)] * 2,
        in_specs=[HBM_SPEC] * 9,
        out_specs=[VMEM_SPEC] * 3,
        scratch_shapes=[pltpu.VMEM((count, rows, columns), BF16) for count, columns in layout.groups]
        + [pltpu.VMEM((count, rank, columns), F32) for count, columns in layout.groups]
        + [
            odd_buffer(layout, rows),
            pltpu.VMEM((layout.matrices, 2 * rank, 2 * rows), F32),
            pltpu.SemaphoreType.DMA((3, slots)),
        ],
        compiler_params=params(12),
        cost_estimate=pl.CostEstimate(flops=8 * rows * rank * layout.columns, bytes_accessed=read, transcendentals=0),
    )(*in_hbm(grads), *in_hbm(errors), *in_hbm(bases))


def take_half(layout, merged):
    def kernel(merged_ref, out_ref):
        out_ref[...] = merged_ref[:, lane_slice((1 - bit_of(0)) * layout.half, layout.half)]

    return add_call("take_half", kernel, [(merged.shape[0], layout.half)], [merged])[0]


def split_sum(layout, merged, received):
    rows = merged.shape[0]

    def kernel(merged_ref, received_ref, out_ref):
        own = bit_of(0) * layout.half
        total = merged_ref[:, lane_slice(own, layout.half)] + received_ref[...]
        out_ref[:rows], out_ref[rows:] = split2(total)

    return pl.pallas_call(
        kernel,
        name="split_sum",
        out_shape=jax.ShapeDtypeStruct((2 * rows, layout.half), BF16),
        in_specs=[VMEM_SPEC] * 2,
        out_specs=VMEM_SPEC,
        compiler_params=params(),
        cost_estimate=pl.CostEstimate(flops=rows * layout.half, bytes_accessed=1_000_000, transcendentals=0),
    )(merged, received)


def next_sum_kernel(layout, step, *refs):
    for part in range(2):
        kept_ref, received_ref = refs[2 * part : 2 * part + 2]
        width = kept_ref.shape[1] // 2
        which = bit_of(layout.orders[part][step])
        for out_ref, pick in zip(refs[4 + 2 * part : 6 + 2 * part], (1 - which, which)):
            where = (slice(None), lane_slice(pick * width, width))
            out_ref[...] = kept_ref[where] + received_ref[where]


def next_sum(layout, step, arrays):
    rows = arrays[0].shape[0]
    return pl.pallas_call(
        functools.partial(next_sum_kernel, layout, step),
        name="next_sum",
        out_shape=[jax.ShapeDtypeStruct((rows, arrays[2 * part].shape[1] // 2), F32) for part in range(2) for _ in range(2)],
        in_specs=[VMEM_SPEC] * 4,
        out_specs=[VMEM_SPEC] * 4,
        compiler_params=params(),
        cost_estimate=pl.CostEstimate(flops=rows * layout.half, bytes_accessed=1_000_000, transcendentals=0),
    )(*arrays)


def add_call(name, kernel, out_shapes, arrays):
    return pl.pallas_call(
        kernel,
        name=name,
        out_shape=[jax.ShapeDtypeStruct(shape, F32) for shape in out_shapes],
        in_specs=[VMEM_SPEC] * len(arrays),
        out_specs=[VMEM_SPEC] * len(out_shapes),
        compiler_params=params(),
        cost_estimate=pl.CostEstimate(
            flops=sum(rows * columns for rows, columns in out_shapes), bytes_accessed=1_000_000, transcendentals=0
        ),
    )(*arrays)


def last_sum(arrays):
    def kernel(*refs):
        for part in range(2):
            refs[4 + part][...] = refs[2 * part][...] + refs[2 * part + 1][...]

    return add_call("last_sum", kernel, [arrays[0].shape, arrays[2].shape], arrays)


def join(layout, step, pieces, received):
    shapes = [(piece.shape[0], 2 * piece.shape[1]) for piece in pieces]

    def kernel(*refs):
        for part in range(2):
            which = bit_of(layout.orders[part][step])
            width = refs[part].shape[1]
            refs[4 + part][:, lane_slice(which * width, width)] = refs[part][...]
            refs[4 + part][:, lane_slice((1 - which) * width, width)] = refs[2 + part][...]

    return add_call("join", kernel, shapes, (*pieces, *received))


def pack(blocks):
    def kernel(*refs):
        column = 0
        for ref in refs[:-1]:
            refs[-1][:, column : column + ref.shape[1]] = ref[...]
            column += ref.shape[1]

    shape = (blocks[0].shape[0], sum(block.shape[1] for block in blocks))
    return add_call("pack", kernel, [shape], blocks)[0]


def orthonormal_rows(product_t, block=4):
    matrices, rank, rows = product_t.shape
    gram = jnp.stack(
        [
            lax.dot_general(
                product_t[j], product_t[j], (((1,), (1,)), ((), ())), precision=lax.Precision.HIGHEST, preferred_element_type=F32
            )
            for j in range(matrices)
        ]
    )
    filler = jnp.zeros((matrices, rank, LANES - rank - rows), F32)
    work = jnp.concatenate([gram, filler, product_t], axis=2)
    done = []
    for first in range(0, rank, block):
        start = first % 8
        row_id = lax.broadcasted_iota(jnp.int32, (1, work.shape[1], 1), 1)
        columns = [jnp.broadcast_to(work[:, :, first + t : first + t + 1], work.shape) for t in range(block)]
        pivot_rows = [work[:, start + t : start + t + 1, :] for t in range(block)]
        scaled = []
        for t in range(block):
            at = start + t
            inverse = 1.0 / columns[t][:, at : at + 1, :]
            scaled.append(pivot_rows[t] * inverse)
            for s in range(t + 1, block):
                pivot_rows[s] = pivot_rows[s] - scaled[t] * columns[t][:, start + s : start + s + 1, :]
                columns[s] = columns[s] - columns[t] * (columns[s][:, at : at + 1, :] * inverse)
        change = columns[0] * scaled[0]
        for t in range(1, block):
            change = change + columns[t] * scaled[t]
        work = work - jnp.where(row_id >= start + block, change, 0.0)
        for t in range(block):
            work = jnp.where(row_id == start + t, pivot_rows[t], work)
        if start + block == 8:
            done.append(work[:, :8, :])
            work = work[:, 8:, :]
    work = jnp.concatenate(done, axis=1)
    row_id = lax.broadcasted_iota(jnp.int32, work.shape, 1)
    lane_id = lax.broadcasted_iota(jnp.int32, work.shape, 2)
    pivots = jnp.sum(jnp.where(row_id == lane_id, work, 0.0), axis=2, keepdims=True)
    return work[:, :, LANES - rows :] * (1.0 / jnp.sqrt(pivots))


def factor_kernel(layout, own_ref, other_ref, sums_ref, left_ref, *refs):
    outs, parts_ref = refs[:-1], refs[-1]
    rows = left_ref.shape[2]
    core = bit_of(0)
    own, other = (jnp.concatenate([ref[:, :, :rows], ref[:, :, rows:]], axis=1) for ref in (own_ref, other_ref))
    both = [jnp.where(core == 0, one, two) for one, two in ((own, other), (other, own))]
    left = orthonormal_rows(jnp.concatenate(both, axis=1))
    left_ref[...] = left
    high, low = split2(left)
    parts_ref[...] = jnp.concatenate([high, high, low], axis=2)
    for cell, (offset, width, part) in enumerate(layout.cells):
        which = bit_of(layout.orders[part][0])
        width //= 2
        for out_ref, pick in zip(outs[2 * cell : 2 * cell + 2], (1 - which, which)):
            begin = offset + pick * width
            for at in range(0, width, layout.granule(cell)):
                column = core * layout.half + begin + at
                matrix = sum((column >= start).astype(jnp.int32) for start in layout.starts[1:])
                value = sums_ref[:, lane_slice(begin + at, layout.granule(cell))]
                stacked = jnp.concatenate([value, value[:rows]], axis=0)
                out_ref[:, at : at + layout.granule(cell)] = dot_plain(parts_ref[matrix], stacked)


def factor(layout, rank, rows, own, other, sums):
    return pl.pallas_call(
        functools.partial(factor_kernel, layout),
        name="factor",
        out_shape=[jax.ShapeDtypeStruct((layout.matrices, rank, rows), F32)]
        + [jax.ShapeDtypeStruct((rank, width // 2), F32) for _, width, _ in layout.cells for _ in range(2)],
        in_specs=[VMEM_SPEC] * 3,
        out_specs=[VMEM_SPEC] * (1 + 2 * len(layout.cells)),
        scratch_shapes=[pltpu.VMEM((layout.matrices, rank, 3 * rows), BF16)],
        compiler_params=params(),
        cost_estimate=pl.CostEstimate(flops=8 * rows * rank * layout.half, bytes_accessed=10_000_000, transcendentals=0),
    )(own, other, sums)


def turn(left):
    matrices, rank, rows = left.shape

    def kernel(left_ref, out_ref):
        high, low = split2(left_ref[...])
        for j in range(matrices):
            parts = jnp.concatenate([high[j], high[j], low[j]], axis=0).astype(F32)
            out_ref[j] = parts.T.astype(BF16)

    return pl.pallas_call(
        kernel,
        name="turn",
        out_shape=pltpu.VMEM((matrices, rows, 3 * rank), BF16),
        in_specs=[VMEM_SPEC],
        out_specs=VMEM_SPEC,
        compiler_params=params(),
        cost_estimate=pl.CostEstimate(flops=100_000, bytes_accessed=100_000, transcendentals=0),
    )(left)


def update_regions(layout, stage):
    regions = []
    for half_core in range(2):
        origin = half_core * layout.half
        if stage == 2:
            regions.append((half_core, None, [(origin, origin + layout.half, None)]))
            continue
        for bits in ((0, 0), (0, 1), (1, 0), (1, 1)):
            ranges = []
            for offset, width, part in layout.cells:
                low = origin + offset + (bits[part] ^ stage) * (width // 2)
                ranges.append((low, low + width // 2, offset // 2))
            regions.append((half_core, bits, ranges))
    return regions


def update_chunks(layout, ranges):
    for low, high, begin in ranges:
        for index, matrix, column, place, width, steps in layout.segments(low, high, 2048):
            for at in range(steps):
                source = None if begin is None else begin + place - low + at * width
                yield index, matrix, column + at * width, place + at * width, width, source


def update_kernel(layout, stage, turned_ref, merged_ref, right_refs, error_refs, basis_refs, right_buf, error_buf, odd_error, odd_basis, sems):
    core = bit_of(0)
    named = [bit_of(layout.orders[part][0]) for part in range(2)]

    def copies_of(chunk, slot):
        index, matrix, column, place, width, _ = chunk
        where = (matrix, slice(None), pl.ds(column, width))
        packed = (slice(None), pl.ds(place, width))
        odd = width % LANES
        error_from = odd_error.at[matrix] if odd else error_buf.at[packed]
        basis_from = odd_basis.at[matrix] if odd else right_buf.at[packed]
        return (
            pltpu.make_async_copy(error_from, error_refs[index].at[(0,) + where], sems.at[0, slot]),
            pltpu.make_async_copy(basis_from, basis_refs[index].at[where], sems.at[1, slot]),
        )

    def run(half_core, ranges):
        if stage == 2:
            for offset, width, part in layout.cells:
                half = width // 2
                source = (slice(None), pl.ds(offset // 2, half))
                values = [ref[source] for ref in right_refs]
                for number in range(2):
                    value = jnp.where(named[part] == number, values[0], values[1])
                    right_buf[:, pl.ds(half_core * layout.half + offset + number * half, half)] = value
        for slot, chunk in enumerate(update_chunks(layout, ranges)):
            index, matrix, _, place, width, source = chunk
            padded = round_up(width, LANES)
            packed = (slice(None), pl.ds(place, padded))
            if stage == 2:
                right = right_buf[packed]
            else:
                right = right_refs[0][:, pl.ds(source, padded)]
                right_buf[packed] = right
            high, low = split2(right)
            approx = dot_plain(turned_ref[layout.firsts[index] + matrix], jnp.concatenate([high, low, high], axis=0))
            error = merged_ref[packed] - approx
            error_buf[packed] = error
            if width < padded:
                odd_error[matrix] = error[:, :width]
                odd_basis[matrix] = right[:, :width]
            for copy in copies_of(chunk, slot):
                copy.start()
        for slot, chunk in enumerate(update_chunks(layout, ranges)):
            for copy in copies_of(chunk, slot):
                copy.wait()

    for half_core, bits, ranges in update_regions(layout, stage):
        if bits is None:
            mine = core != half_core
        else:
            mine = (core == half_core) & (named[0] == bits[0]) & (named[1] == bits[1])
        pl.when(mine)(functools.partial(run, half_core, ranges))


def update_error(layout, rank, stage, turned, merged, rights, before=()):
    rows = merged.shape[0]
    groups = len(layout.groups)
    ins = 2 + len(rights)

    def kernel(*refs):
        turned_ref, merged_ref, *right_refs = refs[:ins]
        refs = refs[ins + len(before) :]
        update_kernel(layout, stage, turned_ref, merged_ref, right_refs, refs[:groups], refs[groups : 2 * groups], *refs[2 * groups :])

    slots = max(len(list(update_chunks(layout, ranges))) for _, _, ranges in update_regions(layout, stage))
    return pl.pallas_call(
        kernel,
        name="update_" + ("first", "own", "other")[stage],
        out_shape=[jax.ShapeDtypeStruct((1, count, rows, columns), F32) for count, columns in layout.groups]
        + [jax.ShapeDtypeStruct((count, rank, columns), F32) for count, columns in layout.groups],
        in_specs=[VMEM_SPEC] * ins + [HBM_SPEC] * len(before),
        out_specs=[HBM_SPEC] * (2 * groups),
        input_output_aliases={ins + number: number for number in range(len(before))},
        scratch_shapes=[
            pltpu.VMEM((rank, layout.packed), F32),
            pltpu.VMEM((rows, layout.packed), F32),
            odd_buffer(layout, rows),
            odd_buffer(layout, rank),
            pltpu.SemaphoreType.DMA((2, slots)),
        ],
        compiler_params=params(12),
        cost_estimate=pl.CostEstimate(flops=100_000, bytes_accessed=40_000_000 if stage else 100_000, transcendentals=0),
    )(turned, merged, *rights, *before)


def swap(value, axis, size, bit):
    return lax.ppermute(value, axis, [(i, i ^ (1 << bit)) for i in range(size)])


def sum_over_bits(value, axis, size, bits):
    while bits:
        turns = [0]
        for bit in bits[:2]:
            turns = turns + [turn | (1 << bit) for turn in turns]
        bits = bits[2:]
        terms = [value] + [lax.ppermute(value, axis, [(i, i ^ turn) for i in range(size)]) for turn in turns[1:]]
        while len(terms) > 1:
            terms = [one + two for one, two in zip(terms[::2], terms[1::2])]
        value = terms[0]
    return value


def per_device(sizes, grad_square, grad_narrow, grad_wide, error_square, error_narrow, error_wide, basis_square, basis_narrow, basis_wide):
    dp, mp = sizes
    dp_bits = dp.bit_length() - 1
    mp_bits = mp.bit_length() - 1
    grads = (grad_square, grad_narrow, grad_wide)
    errors = (error_square, error_narrow, error_wide)
    bases = tuple(jnp.swapaxes(value, 1, 2) for value in (basis_square, basis_narrow, basis_wide))
    rows = grad_square.shape[2]
    rank = basis_square.shape[2]
    layout = Layout([(value.shape[1], value.shape[3]) for value in grads], dp_bits)
    order = lax.optimization_barrier
    steps = dp_bits - 1

    def swap_parts(values, step):
        return [swap(values[part], "dp", dp, layout.orders[part][step]) for part in range(2)]

    merged, send, product = merge_and_project(layout, rank, rows, grads, errors, bases)
    product = product + swap(send, "dp", dp, 0)
    merged, product = order((merged, product))
    received = swap(take_half(layout, merged), "dp", dp, 0)
    product = sum_over_bits(product, "dp", dp, list(range(1, dp_bits)))
    product = sum_over_bits(product, "mp", mp, list(range(mp_bits)))
    received, product = order((received, product))
    sums = split_sum(layout, merged, received)
    left, *arrays = factor(layout, rank, rows, product, swap(product, "dp", dp, 0), sums)
    turned = turn(left)

    chunks = [arrays[4 * chunk : 4 * chunk + 4] for chunk in range(2)]
    for step in range(max(1, steps - 1)):
        traded = [swap_parts(chunk[::2], step) for chunk in chunks]
        chunks = [[chunk[1], one, chunk[3], two] for chunk, (one, two) in zip(chunks, traded)]
        if step < steps - 2:
            chunks = [next_sum(layout, step + 1, chunk) for chunk in chunks]
    chunks = [last_sum(chunk) for chunk in chunks]
    if steps > 1:
        traded = [swap_parts(chunk, steps - 1) for chunk in chunks]
        first = last_sum([chunks[0][0], traded[0][0], chunks[0][1], traded[0][1]])
        one, two = order((*traded[1], *first))[:2]
        chunks = [first, last_sum([chunks[1][0], one, chunks[1][1], two])]
    for step in reversed(range(1, steps - 1)):
        chunks = [join(layout, step, chunk, swap_parts(chunk, step)) for chunk in chunks]
    news = [swap_parts(chunk, 0) for chunk in chunks]
    own = pack([piece for chunk in chunks for piece in chunk])
    first_other = swap(own, "dp", dp, 0)
    outs = update_error(layout, rank, 0, turned, merged, [own])
    tied = order((*outs, *news[0], *news[1]))
    outs, own = tied[: len(outs)], pack(tied[len(outs) :])
    other = swap(own, "dp", dp, 0)
    outs = update_error(layout, rank, 1, turned, merged, [own], outs)
    outs = update_error(layout, rank, 2, turned, merged, [first_other, other], outs)
    return (*outs[:3], *(jnp.swapaxes(value, 1, 2) for value in outs[3:]), jnp.swapaxes(left, 1, 2))


def solution(mesh):
    in_specs = (P("dp", None, None, "mp"),) * 6 + (P(None, "mp", None),) * 3
    out_specs = (P("dp", None, None, "mp"),) * 3 + (P(None, "mp", None),) * 3 + (P(),)
    sizes = (mesh.shape["dp"], mesh.shape["mp"])
    return jax.shard_map(
        functools.partial(per_device, sizes), mesh=mesh, in_specs=in_specs, out_specs=out_specs, check_vma=False
    )
```

```python
import functools
import math

import jax
import jax.numpy as jnp
from jax import lax
from jax.experimental import pallas as pl
from jax.experimental.pallas import tpu as pltpu
from jax.sharding import PartitionSpec as P

LANES = 128
MIB = 1024 * 1024
F32 = jnp.float32
BF16 = jnp.bfloat16


def round_up(value, step):
    return -(-value // step) * step


def chunk_of(columns, most=1024):
    if columns % LANES:
        return columns
    width = min(columns, most) // LANES * LANES
    while columns % width:
        width -= LANES
    return width


def split2(value):
    high = value.astype(BF16)
    low = (value - high.astype(F32)).astype(BF16)
    return high, low


def dot_last(left, right):
    return lax.dot_general(left, right, (((1,), (1,)), ((), ())), preferred_element_type=F32)


def dot_plain(left, right):
    return lax.dot_general(left, right, (((1,), (0,)), ((), ())), preferred_element_type=F32)


def lane_slice(column, width):
    if isinstance(column, int):
        return pl.ds(column, width)
    return pl.ds(pl.multiple_of(column, LANES), width)


class Layout:
    def __init__(self, groups, dp_bits):
        self.groups = groups
        self.places = []
        self.starts = []
        self.firsts = []
        used = 0
        matrices = 0
        for count, columns in groups:
            self.firsts.append(matrices)
            self.places.append(used)
            for _ in range(count):
                self.starts.append(used)
                used += round_up(columns, LANES)
            matrices += count
        self.matrices = matrices
        self.used = used
        unit = 1 << max(1, dp_bits - 2)
        units = max(4, -(-used // (2 * unit * LANES)))
        self.half = units * unit * LANES
        self.packed = 2 * self.half
        self.cells = []
        offset = 0
        base = units // 8
        shares = [2 * base + 2, 2 * base + 2, 2 * base, units - 6 * base - 4]
        if base == 0 or shares[3] < 1:
            shares = [units // 4] * 3 + [units - 3 * (units // 4)]
        for cell, share in enumerate(shares):
            width = share * unit * LANES
            self.cells.append((offset, width, cell % 2))
            offset += width
        self.orders = (list(range(1, dp_bits)), list(range(dp_bits - 1, 0, -1)))
        self.columns = sum(count * columns for count, columns in groups)

    def granule(self, cell):
        offset, width, _ = self.cells[cell]
        return math.gcd(*self.starts, self.half, offset, width // 2)

    def segments(self, low, high, most):
        found = []
        for index, (count, columns) in enumerate(self.groups):
            for matrix in range(count):
                place = self.places[index] + matrix * round_up(columns, LANES)
                begin, end = max(low, place), min(high, place + columns)
                if begin < end:
                    width = chunk_of(end - begin, most)
                    found.append((index, matrix, begin - place, begin, width, (end - begin) // width))
        return found


def widen(value):
    rows, width = value.shape
    if width % LANES == 0:
        return value
    return jnp.concatenate([value, jnp.zeros((rows, round_up(width, LANES) - width), value.dtype)], axis=1)


def bit_of(bit):
    return (lax.axis_index("dp") >> bit) & 1


def params(limit=8):
    return pltpu.CompilerParams(vmem_limit_bytes=limit * MIB)


VMEM_SPEC = pl.BlockSpec(memory_space=pltpu.VMEM)
HBM_SPEC = pl.BlockSpec(memory_space=pltpu.HBM)


def in_hbm(values):
    return [pltpu.with_memory_space_constraint(value, pltpu.HBM) for value in values]


def odd_buffer(layout, rows):
    odd = [(count, columns) for count, columns in layout.groups if columns % LANES] or [(1, LANES)]
    return pltpu.VMEM((max(count for count, _ in odd), rows, max(columns for _, columns in odd)), F32)


def merge_and_project_kernel(layout, grad_refs, error_refs, basis_refs, merged_ref, send_ref, keep_ref, grad_bufs, basis_bufs, odd_ref, total, sems):
    rank = total.shape[1] // 2
    rows = total.shape[2] // 2
    plans = []
    slot = 0
    for segment in layout.segments(0, layout.used, 2048):
        plans.append((*segment, slot))
        slot += segment[-1]

    def copies_of(plan, at):
        index, matrix, column, place, width, _, base = plan
        where = (matrix, slice(None), lane_slice(column + at * width, width))
        error_to = odd_ref.at[matrix] if width % LANES else merged_ref.at[:, lane_slice(place + at * width, width)]
        return (
            pltpu.make_async_copy(grad_refs[index].at[(0,) + where], grad_bufs[index].at[where], sems.at[0, base + at]),
            pltpu.make_async_copy(error_refs[index].at[(0,) + where], error_to, sems.at[1, base + at]),
            pltpu.make_async_copy(basis_refs[index].at[where], basis_bufs[index].at[where], sems.at[2, base + at]),
        )

    for plan in plans:
        for at in range(plan[5]):
            for copy in copies_of(plan, at):
                copy.start()
    if layout.used < layout.packed:
        merged_ref[:, layout.used :] = jnp.zeros((rows, layout.packed - layout.used), F32)
    total[...] = jnp.zeros_like(total)
    for plan in plans:
        index, matrix, column, place, width, steps, _ = plan

        def body(at, carry, plan=plan, index=index, matrix=matrix, column=column, place=place, width=width):
            for copy in copies_of(plan, at):
                copy.wait()
            where = (matrix, slice(None), lane_slice(column + at * width, width))
            packed = (slice(None), lane_slice(place + at * width, round_up(width, LANES)))
            error = odd_ref[matrix] if width % LANES else merged_ref[packed]
            merged = error + grad_bufs[index][where].astype(F32)
            merged_ref[packed] = widen(merged)
            merged_parts = jnp.concatenate(split2(merged), axis=0)
            basis_parts = jnp.concatenate(split2(basis_bufs[index][where]), axis=0)
            total[layout.firsts[index] + matrix] += dot_last(basis_parts, merged_parts)
            return carry

        if steps == 1:
            body(0, 0)
        else:
            lax.fori_loop(0, steps, body, 0)
    core = bit_of(0)
    quarter = rank // 4
    for matrix in range(total.shape[0]):
        value = total[matrix]
        top = value[:rank, :rows] + value[:rank, rows:]
        top = top + (value[rank:, :rows] + value[rank:, rows:])
        quarters = [top[number * quarter : (number + 1) * quarter] for number in range(4)]
        halves = [jnp.concatenate(quarters[2 * half : 2 * half + 2], axis=1) for half in range(2)]
        send_ref[matrix] = jnp.where(core == 0, halves[1], halves[0])
        keep_ref[matrix] = jnp.where(core == 0, halves[0], halves[1])


def merge_and_project(layout, rank, rows, grads, errors, bases):
    def kernel(*refs):
        merge_and_project_kernel(layout, refs[0:3], refs[3:6], refs[6:9], *refs[9:12], refs[12:15], refs[15:18], *refs[18:])

    read = sum(value.size * value.dtype.itemsize for value in (*grads, *errors, *bases))
    slots = sum(segment[-1] for segment in layout.segments(0, layout.used, 2048))
    return pl.pallas_call(
        kernel,
        name="merge_and_project",
        out_shape=[pltpu.VMEM((rows, layout.packed), F32)]
        + [jax.ShapeDtypeStruct((layout.matrices, rank // 4, 2 * rows), F32)] * 2,
        in_specs=[HBM_SPEC] * 9,
        out_specs=[VMEM_SPEC] * 3,
        scratch_shapes=[pltpu.VMEM((count, rows, columns), BF16) for count, columns in layout.groups]
        + [pltpu.VMEM((count, rank, columns), F32) for count, columns in layout.groups]
        + [
            odd_buffer(layout, rows),
            pltpu.VMEM((layout.matrices, 2 * rank, 2 * rows), F32),
            pltpu.SemaphoreType.DMA((3, slots)),
        ],
        compiler_params=params(12),
        cost_estimate=pl.CostEstimate(flops=8 * rows * rank * layout.columns, bytes_accessed=read, transcendentals=0),
    )(*in_hbm(grads), *in_hbm(errors), *in_hbm(bases))


def take_half(layout, merged):
    def kernel(merged_ref, out_ref):
        out_ref[...] = merged_ref[:, lane_slice((1 - bit_of(0)) * layout.half, layout.half)]

    return add_call("take_half", kernel, [(merged.shape[0], layout.half)], [merged])[0]


def split_sum(layout, merged, received):
    rows = merged.shape[0]

    def kernel(merged_ref, received_ref, out_ref):
        own = bit_of(0) * layout.half
        total = merged_ref[:, lane_slice(own, layout.half)] + received_ref[...]
        out_ref[:rows], out_ref[rows:] = split2(total)

    return pl.pallas_call(
        kernel,
        name="split_sum",
        out_shape=jax.ShapeDtypeStruct((2 * rows, layout.half), BF16),
        in_specs=[VMEM_SPEC] * 2,
        out_specs=VMEM_SPEC,
        compiler_params=params(),
        cost_estimate=pl.CostEstimate(flops=rows * layout.half, bytes_accessed=1_000_000, transcendentals=0),
    )(merged, received)


def next_sum_kernel(layout, step, *refs):
    for part in range(2):
        kept_ref, received_ref = refs[2 * part : 2 * part + 2]
        width = kept_ref.shape[1] // 2
        which = bit_of(layout.orders[part][step])
        for out_ref, pick in zip(refs[4 + 2 * part : 6 + 2 * part], (1 - which, which)):
            where = (slice(None), lane_slice(pick * width, width))
            out_ref[...] = kept_ref[where] + received_ref[where]


def next_sum(layout, step, arrays):
    rows = arrays[0].shape[0]
    return pl.pallas_call(
        functools.partial(next_sum_kernel, layout, step),
        name="next_sum",
        out_shape=[jax.ShapeDtypeStruct((rows, arrays[2 * part].shape[1] // 2), F32) for part in range(2) for _ in range(2)],
        in_specs=[VMEM_SPEC] * 4,
        out_specs=[VMEM_SPEC] * 4,
        compiler_params=params(),
        cost_estimate=pl.CostEstimate(flops=rows * layout.half, bytes_accessed=1_000_000, transcendentals=0),
    )(*arrays)


def add_call(name, kernel, out_shapes, arrays):
    return pl.pallas_call(
        kernel,
        name=name,
        out_shape=[jax.ShapeDtypeStruct(shape, F32) for shape in out_shapes],
        in_specs=[VMEM_SPEC] * len(arrays),
        out_specs=[VMEM_SPEC] * len(out_shapes),
        compiler_params=params(),
        cost_estimate=pl.CostEstimate(
            flops=sum(rows * columns for rows, columns in out_shapes), bytes_accessed=1_000_000, transcendentals=0
        ),
    )(*arrays)


def last_sum(arrays):
    def kernel(*refs):
        for part in range(2):
            refs[4 + part][...] = refs[2 * part][...] + refs[2 * part + 1][...]

    return add_call("last_sum", kernel, [arrays[0].shape, arrays[2].shape], arrays)


def join(layout, step, pieces, received):
    shapes = [(piece.shape[0], 2 * piece.shape[1]) for piece in pieces]

    def kernel(*refs):
        for part in range(2):
            which = bit_of(layout.orders[part][step])
            width = refs[part].shape[1]
            refs[4 + part][:, lane_slice(which * width, width)] = refs[part][...]
            refs[4 + part][:, lane_slice((1 - which) * width, width)] = refs[2 + part][...]

    return add_call("join", kernel, shapes, (*pieces, *received))


def pack(blocks):
    def kernel(*refs):
        column = 0
        for ref in refs[:-1]:
            refs[-1][:, column : column + ref.shape[1]] = ref[...]
            column += ref.shape[1]

    shape = (blocks[0].shape[0], sum(block.shape[1] for block in blocks))
    return add_call("pack", kernel, [shape], blocks)[0]


def orthonormal_rows(product_t, block=4):
    matrices, rank, rows = product_t.shape
    gram = jnp.stack(
        [
            lax.dot_general(
                product_t[j], product_t[j], (((1,), (1,)), ((), ())), precision=lax.Precision.HIGHEST, preferred_element_type=F32
            )
            for j in range(matrices)
        ]
    )
    spare = (matrices, rank, LANES - rank - rows)
    filler = (lax.broadcasted_iota(jnp.int32, spare, 1) == lax.broadcasted_iota(jnp.int32, spare, 2)).astype(F32)
    work = jnp.concatenate([gram, filler, product_t], axis=2)
    done = []
    for first in range(0, rank, block):
        start = first % 8
        row_id = lax.broadcasted_iota(jnp.int32, (1, work.shape[1], 1), 1)
        columns = [jnp.broadcast_to(work[:, :, first + t : first + t + 1], work.shape) for t in range(block)]
        pivot_rows = [work[:, start + t : start + t + 1, :] for t in range(block)]
        scaled = []
        for t in range(block):
            at = start + t
            inverse = 1.0 / columns[t][:, at : at + 1, :]
            scaled.append(pivot_rows[t] * inverse)
            for s in range(t + 1, block):
                pivot_rows[s] = pivot_rows[s] - scaled[t] * columns[t][:, start + s : start + s + 1, :]
                columns[s] = columns[s] - columns[t] * (columns[s][:, at : at + 1, :] * inverse)
        change = columns[0] * scaled[0]
        for t in range(1, block):
            change = change + columns[t] * scaled[t]
        work = work - jnp.where(row_id >= start + block, change, 0.0)
        for t in range(block):
            work = jnp.where(row_id == start + t, pivot_rows[t], work)
        if start + block == 8:
            done.append(work[:, :8, :])
            work = work[:, 8:, :]
    work = jnp.concatenate(done, axis=1)
    row_id = lax.broadcasted_iota(jnp.int32, work.shape, 1)
    lane_id = lax.broadcasted_iota(jnp.int32, work.shape, 2)
    pivots = jnp.sum(jnp.where(row_id == lane_id, work, 0.0), axis=2, keepdims=True)
    scale = 1.0 / jnp.sqrt(pivots)
    return work[:, :, LANES - rows :] * scale, work[:, :, rank : 2 * rank] * scale


def project_back_kernel(layout, own_ref, other_ref, sums_ref, product_ref, *refs):
    outs, parts_ref = refs[:-1], refs[-1]
    rows = product_ref.shape[2]
    core = bit_of(0)
    own, other = (jnp.concatenate([ref[:, :, :rows], ref[:, :, rows:]], axis=1) for ref in (own_ref, other_ref))
    both = [jnp.where(core == 0, one, two) for one, two in ((own, other), (other, own))]
    product = jnp.concatenate(both, axis=1)
    product_ref[...] = product
    high, low = split2(product)
    parts_ref[...] = jnp.concatenate([high, high, low], axis=2)
    for cell, (offset, width, part) in enumerate(layout.cells):
        which = bit_of(layout.orders[part][0])
        width //= 2
        for out_ref, pick in zip(outs[2 * cell : 2 * cell + 2], (1 - which, which)):
            begin = offset + pick * width
            for at in range(0, width, layout.granule(cell)):
                column = core * layout.half + begin + at
                matrix = sum((column >= start).astype(jnp.int32) for start in layout.starts[1:])
                value = sums_ref[:, lane_slice(begin + at, layout.granule(cell))]
                stacked = jnp.concatenate([value, value[:rows]], axis=0)
                out_ref[:, at : at + layout.granule(cell)] = dot_plain(parts_ref[matrix], stacked)


def project_back(layout, rank, rows, own, other, sums):
    return pl.pallas_call(
        functools.partial(project_back_kernel, layout),
        name="project_back",
        out_shape=[pltpu.VMEM((layout.matrices, rank, rows), F32)]
        + [jax.ShapeDtypeStruct((rank, width // 2), F32) for _, width, _ in layout.cells for _ in range(2)],
        in_specs=[VMEM_SPEC] * 3,
        out_specs=[VMEM_SPEC] * (1 + 2 * len(layout.cells)),
        scratch_shapes=[pltpu.VMEM((layout.matrices, rank, 3 * rows), BF16)],
        compiler_params=params(),
        cost_estimate=pl.CostEstimate(flops=8 * rows * rank * layout.half, bytes_accessed=10_000_000, transcendentals=0),
    )(own, other, sums)


def factor(product):
    matrices, rank, rows = product.shape

    def kernel(product_ref, left_ref, inverse_ref, turned_ref):
        left, inverse = orthonormal_rows(product_ref[...])
        left_ref[...] = left
        high, low = split2(inverse)
        inverse_ref[...] = jnp.concatenate([high, high, low], axis=2)
        high, low = split2(left)
        for j in range(matrices):
            turned_ref[j] = jnp.concatenate([high[j], high[j], low[j]], axis=0).astype(F32).T.astype(BF16)

    return pl.pallas_call(
        kernel,
        name="factor",
        out_shape=[
            jax.ShapeDtypeStruct((matrices, rank, rows), F32),
            pltpu.VMEM((matrices, rank, 3 * rank), BF16),
            pltpu.VMEM((matrices, rows, 3 * rank), BF16),
        ],
        in_specs=[VMEM_SPEC],
        out_specs=[VMEM_SPEC] * 3,
        compiler_params=params(),
        cost_estimate=pl.CostEstimate(flops=100_000, bytes_accessed=100_000, transcendentals=0),
    )(product)


def finish(layout, chunk, halvings, inverse, arrays):
    def kernel(inverse_ref, *refs):
        for part in range(2):
            kept_ref, received_ref = refs[2 * part : 2 * part + 2]
            cell = 2 * chunk + part
            offset, width, _ = layout.cells[cell]
            first = bit_of(0) * layout.half + offset
            for bit in layout.orders[part][:halvings]:
                width //= 2
                first = first + bit_of(bit) * width
            granule = math.gcd(layout.granule(cell), width)
            for at in range(0, width, granule):
                matrix = sum((first + at >= start).astype(jnp.int32) for start in layout.starts[1:])
                where = (slice(None), slice(at, at + granule))
                high, low = split2(kept_ref[where] + received_ref[where])
                refs[4 + part][where] = dot_plain(inverse_ref[matrix], jnp.concatenate([high, low, high], axis=0))

    return add_call("finish", kernel, [arrays[0].shape, arrays[2].shape], (inverse, *arrays))


def update_regions(layout, stage):
    regions = []
    for half_core in range(2):
        for bits in ((0, 0), (0, 1), (1, 0), (1, 1)):
            ranges = []
            for owner, flip, source in (((0, 0, 0),), ((0, 1, 0), (1, 0, 1)), ((1, 1, 0),))[stage]:
                for offset, width, part in layout.cells:
                    low = (half_core ^ owner) * layout.half + offset + (bits[part] ^ flip) * (width // 2)
                    ranges.append((low, low + width // 2, offset // 2, source))
            regions.append((half_core, bits, ranges))
    return regions


def update_chunks(layout, ranges):
    for low, high, begin, which in ranges:
        for index, matrix, column, place, width, steps in layout.segments(low, high, 2048):
            for at in range(steps):
                source = (which, begin + place - low + at * width)
                yield index, matrix, column + at * width, place + at * width, width, source


def update_kernel(layout, stage, turned_ref, merged_ref, right_refs, error_refs, basis_refs, right_buf, error_buf, odd_error, odd_basis, sems):
    core = bit_of(0)
    named = [bit_of(layout.orders[part][0]) for part in range(2)]

    def copies_of(chunk, slot):
        index, matrix, column, place, width, _ = chunk
        where = (matrix, slice(None), pl.ds(column, width))
        packed = (slice(None), pl.ds(place, width))
        odd = width % LANES
        error_from = odd_error.at[matrix] if odd else error_buf.at[packed]
        basis_from = odd_basis.at[matrix] if odd else right_buf.at[packed]
        return (
            pltpu.make_async_copy(error_from, error_refs[index].at[(0,) + where], sems.at[0, slot]),
            pltpu.make_async_copy(basis_from, basis_refs[index].at[where], sems.at[1, slot]),
        )

    def run(half_core, ranges):
        for slot, chunk in enumerate(update_chunks(layout, ranges)):
            index, matrix, _, place, width, source = chunk
            padded = round_up(width, LANES)
            packed = (slice(None), pl.ds(place, padded))
            right = right_refs[source[0]][:, pl.ds(source[1], padded)]
            right_buf[packed] = right
            high, low = split2(right)
            approx = dot_plain(turned_ref[layout.firsts[index] + matrix], jnp.concatenate([high, low, high], axis=0))
            error = merged_ref[packed] - approx
            error_buf[packed] = error
            if width < padded:
                odd_error[matrix] = error[:, :width]
                odd_basis[matrix] = right[:, :width]
            for copy in copies_of(chunk, slot):
                copy.start()
        for slot, chunk in enumerate(update_chunks(layout, ranges)):
            for copy in copies_of(chunk, slot):
                copy.wait()

    for half_core, bits, ranges in update_regions(layout, stage):
        mine = (core == half_core) & (named[0] == bits[0]) & (named[1] == bits[1])
        pl.when(mine)(functools.partial(run, half_core, ranges))


def update_error(layout, rank, stage, turned, merged, rights, before=()):
    rows = merged.shape[0]
    groups = len(layout.groups)
    ins = 2 + len(rights)

    def kernel(*refs):
        turned_ref, merged_ref, *right_refs = refs[:ins]
        refs = refs[ins + len(before) :]
        update_kernel(layout, stage, turned_ref, merged_ref, right_refs, refs[:groups], refs[groups : 2 * groups], *refs[2 * groups :])

    slots = max(len(list(update_chunks(layout, ranges))) for _, _, ranges in update_regions(layout, stage))
    return pl.pallas_call(
        kernel,
        name="update_" + ("first", "own", "other")[stage],
        out_shape=[jax.ShapeDtypeStruct((1, count, rows, columns), F32) for count, columns in layout.groups]
        + [jax.ShapeDtypeStruct((count, rank, columns), F32) for count, columns in layout.groups],
        in_specs=[VMEM_SPEC] * ins + [HBM_SPEC] * len(before),
        out_specs=[HBM_SPEC] * (2 * groups),
        input_output_aliases={ins + number: number for number in range(len(before))},
        scratch_shapes=[
            pltpu.VMEM((rank, layout.packed), F32),
            pltpu.VMEM((rows, layout.packed), F32),
            odd_buffer(layout, rows),
            odd_buffer(layout, rank),
            pltpu.SemaphoreType.DMA((2, slots)),
        ],
        compiler_params=params(12),
        cost_estimate=pl.CostEstimate(flops=100_000, bytes_accessed=40_000_000 if stage else 100_000, transcendentals=0),
    )(turned, merged, *rights, *before)


def swap(value, axis, size, bit):
    return lax.ppermute(value, axis, [(i, i ^ (1 << bit)) for i in range(size)])


def sum_over_bits(value, axis, size, bits):
    while bits:
        turns = [0]
        for bit in bits[:2]:
            turns = turns + [turn | (1 << bit) for turn in turns]
        bits = bits[2:]
        terms = [value] + [lax.ppermute(value, axis, [(i, i ^ turn) for i in range(size)]) for turn in turns[1:]]
        while len(terms) > 1:
            terms = [one + two for one, two in zip(terms[::2], terms[1::2])]
        value = terms[0]
    return value


def per_device(sizes, grad_square, grad_narrow, grad_wide, error_square, error_narrow, error_wide, basis_square, basis_narrow, basis_wide):
    dp, mp = sizes
    dp_bits = dp.bit_length() - 1
    mp_bits = mp.bit_length() - 1
    grads = (grad_square, grad_narrow, grad_wide)
    errors = (error_square, error_narrow, error_wide)
    bases = tuple(jnp.swapaxes(value, 1, 2) for value in (basis_square, basis_narrow, basis_wide))
    rows = grad_square.shape[2]
    rank = basis_square.shape[2]
    layout = Layout([(value.shape[1], value.shape[3]) for value in grads], dp_bits)
    order = lax.optimization_barrier
    steps = dp_bits - 1

    def swap_parts(values, step):
        return [swap(values[part], "dp", dp, layout.orders[part][step]) for part in range(2)]

    merged, send, product = merge_and_project(layout, rank, rows, grads, errors, bases)
    product = product + swap(send, "dp", dp, 0)
    merged, product = order((merged, product))
    received = swap(take_half(layout, merged), "dp", dp, 0)
    product = sum_over_bits(product, "dp", dp, list(range(1, dp_bits)))
    product = sum_over_bits(product, "mp", mp, list(range(mp_bits)))
    received, product = order((received, product))
    sums = split_sum(layout, merged, received)
    product, *arrays = project_back(layout, rank, rows, product, swap(product, "dp", dp, 0), sums)
    left, inverse, turned = factor(product)

    chunks = [arrays[4 * chunk : 4 * chunk + 4] for chunk in range(2)]
    for step in range(max(1, steps - 1)):
        traded = [swap_parts(chunk[::2], step) for chunk in chunks]
        chunks = [[chunk[1], one, chunk[3], two] for chunk, (one, two) in zip(chunks, traded)]
        if step < steps - 2:
            chunks = [next_sum(layout, step + 1, chunk) for chunk in chunks]
    if steps == 1:
        chunks = [finish(layout, number, 1, inverse, chunk) for number, chunk in enumerate(chunks)]
    else:
        chunks = [last_sum(chunk) for chunk in chunks]
        traded = [swap_parts(chunk, steps - 1) for chunk in chunks]
        first = finish(layout, 0, steps - 1, inverse, [chunks[0][0], traded[0][0], chunks[0][1], traded[0][1]])
        one, two = order((*traded[1], *first))[:2]
        chunks = [first, finish(layout, 1, steps - 1, inverse, [chunks[1][0], one, chunks[1][1], two])]
    for step in reversed(range(1, steps - 1)):
        chunks = [join(layout, step, chunk, swap_parts(chunk, step)) for chunk in chunks]
    news = [swap_parts(chunk, 0) for chunk in chunks]
    own = pack([piece for chunk in chunks for piece in chunk])
    first_other = swap(own, "dp", dp, 0)
    outs = update_error(layout, rank, 0, turned, merged, [own])
    tied = order((*outs, *news[0], *news[1]))
    outs, own = tied[: len(outs)], pack(tied[len(outs) :])
    other = swap(own, "dp", dp, 0)
    outs = update_error(layout, rank, 1, turned, merged, [own, first_other], outs)
    outs = update_error(layout, rank, 2, turned, merged, [other], outs)
    return (*outs[:3], *(jnp.swapaxes(value, 1, 2) for value in outs[3:]), jnp.swapaxes(left, 1, 2))


def solution(mesh):
    in_specs = (P("dp", None, None, "mp"),) * 6 + (P(None, "mp", None),) * 3
    out_specs = (P("dp", None, None, "mp"),) * 3 + (P(None, "mp", None),) * 3 + (P(),)
    sizes = (mesh.shape["dp"], mesh.shape["mp"])
    return jax.shard_map(
        functools.partial(per_device, sizes), mesh=mesh, in_specs=in_specs, out_specs=out_specs, check_vma=False
    )
```
